32 devices in a mesh: member: 8 (over y, x, core), region: 4 (over z).
Axes of the slice: x: 2, y: 2, z: 4, core: 2. Of those that a mesh axis runs over, the one named last changes fastest.
Arguments:
- ensemble: float32 [256, 76, 2048], P('member', None, 'region'), may hold values from -6 to 6
- blending_matrix: float32 [76, 76], replicated, may hold values from -0.625 to 0.625
- lateral_spreading: float32 [76], replicated, may hold values from 0.19 to 0.2
- obs_op: float32 [256, 128, 608], P(('region', 'member')), may hold values from -0.25 to 0.25
- obs_value: float32 [256, 128], P(('region', 'member')), may hold values from -6 to 6
- obs_precision: float32 [256, 128], P(('region', 'member')), may hold values from 0.01 to 3000
Outputs:
- analysis: float32 [256, 76, 2048], P('member', None, 'region')
The draws below stay inside these ranges and needn't reach their ends.
All inputs are finite; a program needn't handle non-finite values.
Results may differ from the reference program's by a relative error of at most 0.0003.
Values sent between devices are 32-bit elements; how exact they have to be, the bound alone decides.
A program may use at most 192 MiB of HBM per device.

```python
import math
from functools import partial
import jax
import jax.numpy as jnp
from jax import lax

ENSEMBLE_SIZE = 256
LAYER_SUM = 76
GY = 128
TILE_WIDTH = 8
NOBS = 128
NSTEP = 4
ITERS = 12
GX = 16
COLS = 2048
TILE_NUMBER = 256
S = 608


def draw_obs_precision(key, part):
    fraction = jax.random.uniform(key, (TILE_NUMBER, NOBS), jnp.float32)
    lowest = -4.605170186
    spread_log = 12.611537754
    values = jnp.exp(lowest + fraction * spread_log)
    return jnp.clip(values, 0.01, 3000.0).astype(jnp.float32)


def block_scale(rng, shape, pieces, smallest, largest):
    factor_of, own = 1.0, jax.random.fold_in(rng, 6)
    for dim, shards_of in pieces:
        steps = jnp.exp(jax.random.uniform(jax.random.fold_in(own, dim), (shards_of,), jnp.float32, smallest / len(pieces), largest / len(pieces)))
        factor_of = factor_of * jnp.repeat(steps, shape[dim] // shards_of).reshape([-1 if axis == dim else 1 for axis in range(len(shape))])
    return factor_of


def scatter_about(own_key, shape, deviation, bound, cuts=(), held_as=jnp.bfloat16):
    gain = block_scale(own_key, shape, cuts, -0.22, 0.18) if cuts else 1.0
    array = jax.random.normal(own_key, shape, jnp.float32) * deviation * gain
    return jnp.minimum(jnp.maximum(array, -bound), bound).astype(held_as)


def setup_inputs(seed: int = 0) -> dict:
    keys = jax.random.split(jax.random.key(seed), 7)
    ensemble = scatter_about(keys[0], (ENSEMBLE_SIZE, LAYER_SUM, COLS), 1.0, 6.0, ((0, 8), (2, 4)), jnp.float32)
    blending_matrix = scatter_about(keys[1], (LAYER_SUM, LAYER_SUM), LAYER_SUM ** -0.5, 0.625, (), jnp.float32)
    lateral_spreading = jnp.clip(jax.random.uniform(keys[2], (LAYER_SUM,), jnp.float32, 0.19, 0.2), 0.19, 0.2)
    obs_op = scatter_about(keys[3], (TILE_NUMBER, NOBS, S), S ** -0.5, 0.25, ((0, 32),), jnp.float32)
    obs_value = scatter_about(keys[4], (TILE_NUMBER, NOBS), 1.0, 6.0, ((0, 32),), jnp.float32)
    obs_precision = draw_obs_precision(jax.random.fold_in(keys[6], 71), 0)
    return dict(ensemble=ensemble, blending_matrix=blending_matrix, lateral_spreading=lateral_spreading, obs_op=obs_op, obs_value=obs_value, obs_precision=obs_precision)


HIGHEST = lax.Precision.HIGHEST

def realisation_prediction(layered_variables, blending_matrix, lateral_spreading):
    for step_index in range(NSTEP):
        laplace = jnp.roll(layered_variables, -1, 1) + jnp.roll(layered_variables, 1, 1) + jnp.roll(layered_variables, -1, 2) + jnp.roll(layered_variables, 1, 2) - 4.0 * layered_variables
        coupled = jnp.einsum('fg,gxy->fxy', blending_matrix, layered_variables, precision=HIGHEST)
        layered_variables = layered_variables + lateral_spreading[:, None, None] * laplace + 0.3 * jnp.tanh(coupled)
    return layered_variables

def analyse(packed):
    patch_state, operator, observed, precisions = packed
    mean_state = lax.optimization_barrier(jnp.mean(patch_state, axis=0))
    perturb = patch_state - mean_state
    obs_pert = jnp.dot(perturb, operator.T, precision=HIGHEST, preferred_element_type=jnp.float32)
    obs_mean = jnp.dot(operator, mean_state, precision=HIGHEST, preferred_element_type=jnp.float32)
    innovation = observed - obs_mean
    weighted = obs_pert * precisions
    gram_matrix = jnp.dot(weighted, obs_pert.T, precision=HIGHEST, preferred_element_type=jnp.float32)
    identity = jnp.eye(ENSEMBLE_SIZE, dtype=jnp.float32)
    system = (ENSEMBLE_SIZE - 1.0) * identity + gram_matrix
    norm_scale = jnp.sqrt(jnp.sum(system * system))
    sqrt_iter = system / norm_scale
    inv_iter = identity
    for step_index in range(ITERS):
        factor = 0.5 * (3.0 * identity - jnp.dot(inv_iter, sqrt_iter, precision=HIGHEST, preferred_element_type=jnp.float32))
        sqrt_iter = jnp.dot(sqrt_iter, factor, precision=HIGHEST, preferred_element_type=jnp.float32)
        inv_iter = jnp.dot(factor, inv_iter, precision=HIGHEST, preferred_element_type=jnp.float32)
    inv_sqrt = inv_iter / jnp.sqrt(norm_scale)
    inverse = jnp.dot(inv_sqrt, inv_sqrt, precision=HIGHEST, preferred_element_type=jnp.float32)
    mean_w = jnp.dot(inverse, jnp.dot(weighted, innovation, precision=HIGHEST, preferred_element_type=jnp.float32), precision=HIGHEST, preferred_element_type=jnp.float32)
    weights = math.sqrt(ENSEMBLE_SIZE - 1.0) * inv_sqrt + mean_w[:, None]
    return mean_state + jnp.dot(weights.T, perturb, precision=HIGHEST, preferred_element_type=jnp.float32)

def reference(ensemble, blending_matrix, lateral_spreading, obs_op, obs_value, obs_precision):
    realisation_lattice = ensemble.reshape(ENSEMBLE_SIZE, LAYER_SUM, GX, GY)
    predict_advance = lax.map(partial(realisation_prediction, blending_matrix=blending_matrix, lateral_spreading=lateral_spreading), realisation_lattice)
    neighbourhood_tiles = predict_advance.reshape(ENSEMBLE_SIZE, LAYER_SUM, TILE_NUMBER, TILE_WIDTH).transpose(2, 0, 1, 3).reshape(TILE_NUMBER, ENSEMBLE_SIZE, LAYER_SUM * TILE_WIDTH)
    result = lax.map(analyse, (neighbourhood_tiles, obs_op, obs_value, obs_precision))
    return result.reshape(TILE_NUMBER, ENSEMBLE_SIZE, LAYER_SUM, TILE_WIDTH).transpose(1, 2, 0, 3).reshape(ENSEMBLE_SIZE, LAYER_SUM, COLS)
```

```python
import functools
import math

import jax
import jax.numpy as jnp
from jax import lax
from jax.experimental import pallas as pl
from jax.experimental.pallas import tpu as pltpu
from jax.sharding import PartitionSpec as P

GY = 128
NSTEP = 4
ITERS = 12
HIGHEST = lax.Precision.HIGHEST
F32 = jnp.float32
BF16 = jnp.bfloat16
VMEM = pl.BlockSpec(memory_space=pltpu.VMEM)
PARAMS = pltpu.CompilerParams(vmem_limit_bytes=56 * 2**20)


def mm(a, b):
    return jnp.dot(a, b, preferred_element_type=F32)


def split2(x):
    hi = x.astype(BF16)
    return hi, (x - hi.astype(F32)).astype(BF16)


def split3(x):
    hi = x.astype(BF16)
    rest = x - hi.astype(F32)
    mid = rest.astype(BF16)
    return hi, mid, (rest - mid.astype(F32)).astype(BF16)


def dot3(a, b):
    a0, a1 = split2(a)
    b0, b1 = split2(b)
    return mm(a0, b0) + (mm(a0, b1) + mm(a1, b0))


def dot6(a, b):
    a0, a1, a2 = split3(a)
    b0, b1, b2 = split3(b)
    left = jnp.concatenate([a0, a1], 1)
    low = mm(jnp.concatenate([a0, a2], 1), jnp.concatenate([b2, b0], 0))
    low = low + mm(left, jnp.concatenate([b1, b0], 0))
    return low + mm(left, jnp.concatenate([b0, b1], 0))


def mixing(blend_ref, levels):
    padded = blend_ref.shape[0]
    hi, lo = split2(blend_ref[...])
    lane = lax.broadcasted_iota(jnp.int32, blend_ref.shape, 1)
    return jnp.where(lane < 2 * padded, hi.astype(F32), lo.astype(F32)).astype(BF16)


def advance(x, up, down, mix, rate):
    levels = x.shape[0]
    padded = mix.shape[0]
    full = jnp.concatenate([x, jnp.zeros((padded - levels, x.shape[1]), F32)], 0)
    hi, lo = split2(full)
    coupled = mm(mix, jnp.concatenate([hi, lo, hi], 0))[:levels]
    rows = x.shape[1] // GY
    parts = [x[:, r * GY:(r + 1) * GY] for r in range(rows)]
    ext = [up] + parts + [down]
    out = []
    for r in range(rows):
        c = parts[r]
        lap = ext[r] + ext[r + 2] + pltpu.roll(c, 1, 1) + pltpu.roll(c, GY - 1, 1) - 4.0 * c
        out.append(c + rate * lap + 0.3 * jnp.tanh(coupled[:, r * GY:(r + 1) * GY]))
    return out


def step_kernel(x_ref, up_ref, down_ref, blend_ref, rate_ref, o_ref, head_ref, tail_ref):
    levels = x_ref.shape[1]
    mix = mixing(blend_ref, levels)
    rate = rate_ref[...]

    @pl.loop(0, x_ref.shape[0])
    def _(m):
        new = advance(x_ref[m], up_ref[m], down_ref[m], mix, rate)
        for r, part in enumerate(new):
            o_ref[m, :, r * GY:(r + 1) * GY] = part
        head_ref[m] = new[0]
        tail_ref[m] = new[-1]


def rows_of(i, levels, stride):
    return pl.ds(i, levels) if stride == 1 else pl.ds(i, levels, stride=stride)


def last_kernel(x_ref, up_ref, down_ref, blend_ref, rate_ref, o_ref):
    mem, levels, cols = x_ref.shape
    rows = cols // GY
    pack = o_ref.shape[0] // rows
    width = GY // pack
    group = mem // pack
    mix = mixing(blend_ref, levels)
    rate = rate_ref[...]
    place = lax.broadcasted_iota(jnp.int32, (levels, GY), 1) // width

    def body(i):
        news = []
        for h in range(pack):
            m = h * group + i
            news.append(advance(x_ref[m], up_ref[m], down_ref[m], mix, rate))
        for r in range(rows):
            for c in range(pack):
                value = news[c][r]
                for h in range(pack):
                    if h != c:
                        moved = pltpu.roll(news[h][r], (h - c) * width % GY, 1)
                        value = jnp.where(place == h, moved, value)
                o_ref[r * pack + c, rows_of(i, levels, group), :] = value

    if group == 1:
        body(0)
    else:
        pl.loop(0, group)(body)


def unpack_kernel(x_ref, o_ref):
    mem, levels, cols = o_ref.shape
    rows = cols // GY
    pack = x_ref.shape[0] // rows
    width = GY // pack
    group = mem // pack
    place = lax.broadcasted_iota(jnp.int32, (levels, GY), 1) // width

    def body(i):
        for r in range(rows):
            got = [x_ref[r * pack + c, rows_of(i, levels, group), :] for c in range(pack)]
            for h in range(pack):
                value = got[h]
                for c in range(pack):
                    if c != h:
                        value = jnp.where(place == c, pltpu.roll(got[c], (c - h) * width % GY, 1), value)
                o_ref[h * group + i, :, r * GY:(r + 1) * GY] = value

    if group == 1:
        body(0)
    else:
        pl.loop(0, group)(body)


def analysis_kernel(levels, x_ref, op_ref, val_ref, prec_ref, o_ref,
                    xt_ref, mean_ref, u_ref, v_ref, state_ref, scal_ref):
    sources, packed, _ = x_ref.shape
    group = packed // levels
    patches, nobs, entries = op_ref.shape
    cells = entries // levels
    ens = xt_ref.shape[2]
    width = patches * cells
    pack = GY // width
    half = sources * group
    a = ens - 1.0
    eye = (lax.broadcasted_iota(jnp.int32, (nobs, nobs), 0)
           == lax.broadcasted_iota(jnp.int32, (nobs, nobs), 1)).astype(F32)

    @pl.loop(0, levels)
    def _(f):
        if group == 1:
            x = x_ref[:, f, :]
        else:
            x = x_ref[:, pl.ds(pl.multiple_of(f * group, group), group), :].reshape(half, GY)
        t = x.T
        for h in range(pack):
            for p in range(patches):
                xt_ref[p, pl.ds(pl.multiple_of(f * cells, cells), cells), h * half:(h + 1) * half] = (
                    t[h * width + p * cells:h * width + (p + 1) * cells, :])

    @pl.loop(0, patches)
    def _(p):
        x = xt_ref[p]
        mean = jnp.sum(x, axis=1, keepdims=True) * (1.0 / ens)
        e = x - mean
        xt_ref[p] = e
        mean_ref[p] = mean
        op = op_ref[p]
        obs_mean = jnp.dot(op, jnp.broadcast_to(mean, (entries, GY)), precision=HIGHEST,
                           preferred_element_type=F32)[:, :1]
        root = jnp.sqrt(prec_ref[p])
        u = dot3(op, e) * root
        u_ref[p] = u
        v_ref[p] = root * (val_ref[p] - obs_mean)
        gram = lax.dot_general(u, u, (((1,), (1,)), ((), ())), precision=HIGHEST,
                               preferred_element_type=F32)
        trace = jnp.sum(u * u, keepdims=True).reshape(1, 1)
        square = jnp.sum(gram * gram, keepdims=True).reshape(1, 1)
        s = jnp.sqrt(a * a * ens + 2.0 * a * trace + square)
        alpha = a / s
        state_ref[p, :, 0:nobs] = alpha * eye + gram / s
        state_ref[p, :, nobs:2 * nobs] = eye
        state_ref[p, :, 2 * nobs:3 * nobs] = jnp.zeros_like(eye)
        scal_ref[p, 0:1, :] = jnp.broadcast_to(s, (1, GY))
        scal_ref[p, 1:2, :] = jnp.broadcast_to(alpha, (1, GY))
        scal_ref[p, 2:3, :] = jnp.ones((1, GY), F32)

    @pl.loop(0, ITERS)
    def _(k):
        firsts = []
        for p in range(patches):
            state = state_ref[p]
            firsts.append(dot6(state[:, nobs:2 * nobs], state))
        for p in range(patches):
            first = firsts[p]
            alpha = scal_ref[p, 1:2, 0:1]
            z = scal_ref[p, 2:3, 0:1]
            factor = 1.5 * eye - 0.5 * first[:, 0:nobs]
            second = dot6(factor, state_ref[p])
            state_ref[p, :, 0:2 * nobs] = second[:, 0:2 * nobs]
            q = state_ref[p, :, 2 * nobs:3 * nobs]
            state_ref[p, :, 2 * nobs:3 * nobs] = second[:, 2 * nobs:3 * nobs] - 0.5 * z * (
                first[:, nobs:2 * nobs] + alpha * (first[:, 2 * nobs:3 * nobs] + z * q))
            scal_ref[p, 2:3, :] = jnp.broadcast_to(z * (1.5 - 0.5 * alpha * z * z), (1, GY))

    @pl.loop(0, patches)
    def _(p):
        s = scal_ref[p, 0:1, 0:1]
        z = scal_ref[p, 2:3, 0:1]
        scale = lax.rsqrt(s)
        root = state_ref[p, :, nobs:2 * nobs] * scale
        u = u_ref[p]
        once = jnp.sum(root * v_ref[p], axis=0, keepdims=True)
        twice = jnp.sum(root * once, axis=1, keepdims=True)
        w = jnp.sum(u * twice, axis=0, keepdims=True)
        e = xt_ref[p]
        qu = dot3(state_ref[p, :, 2 * nobs:3 * nobs], u) * (math.sqrt(a) * scale / s)
        weights = dot3(u.T, qu)
        shift = mean_ref[p] + jnp.sum(e * w, axis=1, keepdims=True)
        xt_ref[p] = shift + (math.sqrt(a) * scale * z) * e + dot3(e, weights)

    @pl.loop(0, levels)
    def _(f):
        t = jnp.concatenate([
            xt_ref[p, pl.ds(pl.multiple_of(f * cells, cells), cells), h * half:(h + 1) * half]
            for h in range(pack) for p in range(patches)], 0).T
        if group == 1:
            o_ref[:, f, :] = t
        else:
            o_ref[:, pl.ds(pl.multiple_of(f * group, group), group), :] = t.reshape(
                sources, group, GY)


def call(kernel, outs, args, scratch=(), params=PARAMS):
    return pl.pallas_call(
        kernel,
        out_shape=[jax.ShapeDtypeStruct(s, F32) for s in outs],
        in_specs=[VMEM] * len(args),
        out_specs=[VMEM] * len(outs),
        scratch_shapes=list(scratch),
        compiler_params=params,
    )(*args)


def shards(ensemble, blending_matrix, lateral_spreading, obs_op, obs_value, obs_precision):
    mem, levels, cols = ensemble.shape
    members = lax.axis_size("member")
    regions = lax.axis_size("region")
    patches, nobs, entries = obs_op.shape
    ens = mem * members
    pack = GY * members // cols
    padded = -(-levels // 16) * 16
    blend = jnp.tile(jnp.pad(blending_matrix, ((0, padded - levels),) * 2), (1, 3))
    rate = lateral_spreading[:, None]
    x, head, tail = ensemble, ensemble[:, :, :GY], ensemble[:, :, -GY:]
    for step in range(NSTEP):
        up = lax.ppermute(tail, "region", [(i, (i + 1) % regions) for i in range(regions)])
        down = lax.ppermute(head, "region", [((i + 1) % regions, i) for i in range(regions)])
        args = (x, up, down, blend, rate)
        if step < NSTEP - 1:
            side = (mem, levels, GY)
            x, head, tail = call(step_kernel, [x.shape, side, side], args)
    packed = (members, levels * mem // pack, GY)
    out, = call(last_kernel, [packed], args)
    got = lax.all_to_all(out, "member", split_axis=0, concat_axis=0, tiled=True)
    back, = call(
        functools.partial(analysis_kernel, levels), [packed],
        (got, obs_op, obs_value[:, :, None], obs_precision[:, :, None]),
        [
            pltpu.VMEM((patches, entries, ens), F32),
            pltpu.VMEM((patches, entries, 1), F32),
            pltpu.VMEM((patches, nobs, ens), F32),
            pltpu.VMEM((patches, nobs, 1), F32),
            pltpu.VMEM((patches, nobs, 3 * nobs), F32),
            pltpu.VMEM((patches, 8, GY), F32),
        ])
    back = lax.all_to_all(back, "member", split_axis=0, concat_axis=0, tiled=True)
    return call(unpack_kernel, [ensemble.shape], (back,))[0]


def solution(mesh):
    return jax.shard_map(
        shards,
        mesh=mesh,
        in_specs=(
            P("member", None, "region"),
            P(),
            P(),
            P(("region", "member"), None, None),
            P(("region", "member"), None),
            P(("region", "member"), None),
        ),
        out_specs=P("member", None, "region"),
        check_vma=False,
    )
```

```python
import functools
import math

import jax
import jax.numpy as jnp
from jax import lax
from jax.experimental import pallas as pl
from jax.experimental.pallas import tpu as pltpu
from jax.sharding import PartitionSpec as P

GY = 128
NSTEP = 4
ITERS = 12
HIGHEST = lax.Precision.HIGHEST
F32 = jnp.float32
BF16 = jnp.bfloat16
VMEM = pl.BlockSpec(memory_space=pltpu.VMEM)
PARAMS = pltpu.CompilerParams(vmem_limit_bytes=56 * 2**20)


def mm(a, b):
    return jnp.dot(a, b, preferred_element_type=F32)


def split2(x):
    hi = x.astype(BF16)
    return hi, (x - hi.astype(F32)).astype(BF16)


def split3(x):
    hi = x.astype(BF16)
    rest = x - hi.astype(F32)
    mid = rest.astype(BF16)
    return hi, mid, (rest - mid.astype(F32)).astype(BF16)


def dot3(a, b):
    a0, a1 = split2(a)
    b0, b1 = split2(b)
    return mm(a0, b0) + (mm(a0, b1) + mm(a1, b0))


def dot6(a, b):
    a0, a1, a2 = split3(a)
    b0, b1, b2 = split3(b)
    left = jnp.concatenate([a0, a1], 1)
    low = mm(jnp.concatenate([a0, a2], 1), jnp.concatenate([b2, b0], 0))
    low = low + mm(left, jnp.concatenate([b1, b0], 0))
    return low + mm(left, jnp.concatenate([b0, b1], 0))


def mixing(blend_ref, levels):
    padded = blend_ref.shape[0]
    hi, lo = split2(blend_ref[...])
    lane = lax.broadcasted_iota(jnp.int32, blend_ref.shape, 1)
    return jnp.where(lane < 2 * padded, hi.astype(F32), lo.astype(F32)).astype(BF16)


def advance(parts, up, down, mix, rate):
    x = jnp.concatenate(parts, 1)
    levels = x.shape[0]
    padded = mix.shape[0]
    full = jnp.concatenate([x, jnp.zeros((padded - levels, x.shape[1]), F32)], 0)
    hi, lo = split2(full)
    coupled = mm(mix, jnp.concatenate([hi, lo, hi], 0))[:levels]
    rows = x.shape[1] // GY
    ext = [up] + parts + [down]
    out = []
    for r in range(rows):
        c = parts[r]
        lap = ext[r] + ext[r + 2] + pltpu.roll(c, 1, 1) + pltpu.roll(c, GY - 1, 1) - 4.0 * c
        out.append(c + rate * lap + 0.3 * jnp.tanh(coupled[:, r * GY:(r + 1) * GY]))
    return out


def rows_of(i, levels, stride):
    return pl.ds(0, levels) if stride == 1 else pl.ds(i, levels, stride=stride)


def groups_of(group):
    count = max(1, group // 8)
    return count, group // count


def others(axis):
    count = lax.axis_size(axis)
    me = lax.axis_index(axis)
    return me, [lax.rem(me + j, count) for j in range(1, count)]


def forecast_kernel(ens_ref, blend_ref, rate_ref, o_ref, x_ref, up_ref, down_ref, pack_ref,
                    load_sem, halo_send, halo_recv, part_send, part_recv, own_sem):
    rows, count, pack, size, levels, _ = x_ref.shape
    width = GY // pack
    me, peers = others("member")
    regions = lax.axis_size("region")
    here = lax.axis_index("region")
    above = lax.rem(here + 1, regions)
    below = lax.rem(here + regions - 1, regions)

    loads = {}
    for g in range(count):
        for r in range(rows):
            for h in range(pack):
                first = (h * count + g) * size
                loads[g, r, h] = pltpu.make_async_copy(
                    ens_ref.at[pl.ds(first, size), :, pl.ds(r * GY, GY)],
                    x_ref.at[r, g, h], load_sem.at[g, r, h])
                loads[g, r, h].start()

    barrier = pltpu.get_barrier_semaphore()
    for other in peers:
        pl.semaphore_signal(barrier, inc=1, device_id={"member": other},
                            device_id_type=pl.DeviceIdType.MESH)
    for other in (above, below):
        pl.semaphore_signal(barrier, inc=1, device_id={"region": other},
                            device_id_type=pl.DeviceIdType.MESH)
    pl.semaphore_wait(barrier, len(peers) + 2)

    def halos(k, g):
        return [
            pltpu.make_async_remote_copy(
                src_ref=x_ref.at[r, g], dst_ref=ref.at[k, g],
                send_sem=halo_send.at[side, k, g], recv_sem=halo_recv.at[side, k, g],
                device_id={"region": other}, device_id_type=pl.DeviceIdType.MESH)
            for side, (r, ref, other) in enumerate(
                ((rows - 1, up_ref, above), (0, down_ref, below)))
        ]

    def part(g, j):
        return pltpu.make_async_remote_copy(
            src_ref=pack_ref.at[peers[j], g], dst_ref=o_ref.at[me, g],
            send_sem=part_send.at[g, j], recv_sem=part_recv.at[g, j],
            device_id={"member": peers[j]}, device_id_type=pl.DeviceIdType.MESH)

    mix = mixing(blend_ref, levels)
    rate = rate_ref[...]
    place = lax.broadcasted_iota(jnp.int32, (levels, GY), 1) // width

    for g in range(count):
        for r in range(rows):
            for h in range(pack):
                loads[g, r, h].wait()
        for copy in halos(0, g):
            copy.start()
    for k in range(NSTEP):
        for g in range(count):
            for copy in halos(k, g):
                copy.wait()

            @pl.loop(0, size)
            def _(i):
                news = []
                for h in range(pack):
                    new = advance([x_ref[r, g, h, i] for r in range(rows)],
                                  up_ref[k, g, h, i], down_ref[k, g, h, i], mix, rate)
                    news.append(new)
                    if k < NSTEP - 1:
                        for r in range(rows):
                            x_ref[r, g, h, i] = new[r]
                if k == NSTEP - 1:
                    for r in range(rows):
                        for c in range(pack):
                            value = news[c][r]
                            for h in range(pack):
                                if h != c:
                                    moved = pltpu.roll(news[h][r], (h - c) * width % GY, 1)
                                    value = jnp.where(place == h, moved, value)
                            pack_ref[r * pack + c, g, rows_of(i, levels, size), :] = value

            if k < NSTEP - 1:
                for copy in halos(k + 1, g):
                    copy.start()
            else:
                for j in range(len(peers)):
                    part(g, j).start()
                pltpu.make_async_copy(pack_ref.at[me, g], o_ref.at[me, g], own_sem.at[g]).start()
    for g in range(count):
        for j in range(len(peers)):
            part(g, j).wait()
        pltpu.make_async_copy(pack_ref.at[me, g], o_ref.at[me, g], own_sem.at[g]).wait()


def unpack_kernel(x_ref, o_ref):
    mem, levels, cols = o_ref.shape
    rows = cols // GY
    pack = x_ref.shape[0] // rows
    width = GY // pack
    count, size = groups_of(mem // pack)
    place = lax.broadcasted_iota(jnp.int32, (levels, GY), 1) // width

    for g in range(count):
        @pl.loop(0, size)
        def _(i):
            for r in range(rows):
                got = [x_ref[r * pack + c, g, rows_of(i, levels, size), :] for c in range(pack)]
                for h in range(pack):
                    value = got[h]
                    for c in range(pack):
                        if c != h:
                            value = jnp.where(place == c, pltpu.roll(got[c], (c - h) * width % GY, 1), value)
                    o_ref[(h * count + g) * size + i, :, r * GY:(r + 1) * GY] = value


def analysis_kernel(levels, x_ref, op_ref, val_ref, prec_ref, o_ref,
                    xt_ref, mean_ref, u_ref, v_ref, state_ref, scal_ref):
    sources, count, packed, _ = x_ref.shape
    size = packed // levels
    patches, nobs, entries = op_ref.shape
    cells = entries // levels
    ens = xt_ref.shape[2]
    width = patches * cells
    pack = GY // width
    share = sources * size
    half = count * share
    a = ens - 1.0
    eye = (lax.broadcasted_iota(jnp.int32, (nobs, nobs), 0)
           == lax.broadcasted_iota(jnp.int32, (nobs, nobs), 1)).astype(F32)

    @pl.loop(0, levels)
    def _(f):
        if size == 1:
            x = [x_ref[:, g, f, :] for g in range(count)]
        else:
            x = [x_ref[:, g, pl.ds(pl.multiple_of(f * size, size), size), :].reshape(share, GY)
                 for g in range(count)]
        t = jnp.concatenate(x, 0).T
        for h in range(pack):
            for p in range(patches):
                xt_ref[p, pl.ds(pl.multiple_of(f * cells, cells), cells), h * half:(h + 1) * half] = (
                    t[h * width + p * cells:h * width + (p + 1) * cells, :])

    @pl.loop(0, patches)
    def _(p):
        x = xt_ref[p]
        mean = jnp.sum(x, axis=1, keepdims=True) * (1.0 / ens)
        e = x - mean
        xt_ref[p] = e
        mean_ref[p] = mean
        op = op_ref[p]
        obs_mean = jnp.dot(op, jnp.broadcast_to(mean, (entries, GY)), precision=HIGHEST,
                           preferred_element_type=F32)[:, :1]
        root = jnp.sqrt(prec_ref[p])
        u = dot3(op, e) * root
        u_ref[p] = u
        v_ref[p] = root * (val_ref[p] - obs_mean)
        gram = lax.dot_general(u, u, (((1,), (1,)), ((), ())), precision=HIGHEST,
                               preferred_element_type=F32)
        trace = jnp.sum(u * u, keepdims=True).reshape(1, 1)
        square = jnp.sum(gram * gram, keepdims=True).reshape(1, 1)
        s = jnp.sqrt(a * a * ens + 2.0 * a * trace + square)
        alpha = a / s
        state_ref[p, :, 0:nobs] = alpha * eye + gram / s
        state_ref[p, :, nobs:2 * nobs] = eye
        state_ref[p, :, 2 * nobs:3 * nobs] = jnp.zeros_like(eye)
        scal_ref[p, 0:1, :] = jnp.broadcast_to(s, (1, GY))
        scal_ref[p, 1:2, :] = jnp.broadcast_to(alpha, (1, GY))
        scal_ref[p, 2:3, :] = jnp.ones((1, GY), F32)

    @pl.loop(0, ITERS)
    def _(k):
        firsts = []
        for p in range(patches):
            state = state_ref[p]
            firsts.append(dot6(state[:, nobs:2 * nobs], state))
        for p in range(patches):
            first = firsts[p]
            alpha = scal_ref[p, 1:2, 0:1]
            z = scal_ref[p, 2:3, 0:1]
            factor = 1.5 * eye - 0.5 * first[:, 0:nobs]
            second = dot6(factor, state_ref[p])
            state_ref[p, :, 0:2 * nobs] = second[:, 0:2 * nobs]
            q = state_ref[p, :, 2 * nobs:3 * nobs]
            state_ref[p, :, 2 * nobs:3 * nobs] = second[:, 2 * nobs:3 * nobs] - 0.5 * z * (
                first[:, nobs:2 * nobs] + alpha * (first[:, 2 * nobs:3 * nobs] + z * q))
            scal_ref[p, 2:3, :] = jnp.broadcast_to(z * (1.5 - 0.5 * alpha * z * z), (1, GY))

    @pl.loop(0, patches)
    def _(p):
        s = scal_ref[p, 0:1, 0:1]
        z = scal_ref[p, 2:3, 0:1]
        scale = lax.rsqrt(s)
        root = state_ref[p, :, nobs:2 * nobs] * scale
        u = u_ref[p]
        once = jnp.sum(root * v_ref[p], axis=0, keepdims=True)
        twice = jnp.sum(root * once, axis=1, keepdims=True)
        w = jnp.sum(u * twice, axis=0, keepdims=True)
        e = xt_ref[p]
        qu = dot3(state_ref[p, :, 2 * nobs:3 * nobs], u) * (math.sqrt(a) * scale / s)
        weights = dot3(u.T, qu)
        shift = mean_ref[p] + jnp.sum(e * w, axis=1, keepdims=True)
        xt_ref[p] = shift + (math.sqrt(a) * scale * z) * e + dot3(e, weights)

    @pl.loop(0, levels)
    def _(f):
        t = jnp.concatenate([
            xt_ref[p, pl.ds(pl.multiple_of(f * cells, cells), cells), h * half:(h + 1) * half]
            for h in range(pack) for p in range(patches)], 0).T
        for g in range(count):
            mine = t[g * share:(g + 1) * share]
            if size == 1:
                o_ref[:, g, f, :] = mine
            else:
                o_ref[:, g, pl.ds(pl.multiple_of(f * size, size), size), :] = mine.reshape(
                    sources, size, GY)


def call(kernel, outs, args, scratch=(), params=PARAMS, specs=None):
    return pl.pallas_call(
        kernel,
        out_shape=[jax.ShapeDtypeStruct(s, F32) for s in outs],
        in_specs=specs or [VMEM] * len(args),
        out_specs=[VMEM] * len(outs),
        scratch_shapes=list(scratch),
        compiler_params=params,
    )(*args)


def shards(ensemble, blending_matrix, lateral_spreading, obs_op, obs_value, obs_precision):
    mem, levels, cols = ensemble.shape
    members = lax.axis_size("member")
    patches, nobs, entries = obs_op.shape
    ens = mem * members
    rows = cols // GY
    pack = GY * members // cols
    count, size = groups_of(mem // pack)
    padded = -(-levels // 16) * 16
    blend = jnp.tile(jnp.pad(blending_matrix, ((0, padded - levels),) * 2), (1, 3))
    rate = lateral_spreading[:, None]
    packed = (members, count, levels * size, GY)
    dma = pltpu.SemaphoreType.DMA
    got, = call(
        forecast_kernel, [packed], (ensemble, blend, rate),
        [
            pltpu.VMEM((rows, count, pack, size, levels, GY), F32),
            pltpu.VMEM((NSTEP, count, pack, size, levels, GY), F32),
            pltpu.VMEM((NSTEP, count, pack, size, levels, GY), F32),
            pltpu.VMEM(packed, F32),
            dma((count, rows, pack)),
            dma((2, NSTEP, count)),
            dma((2, NSTEP, count)),
            dma((count, members - 1)),
            dma((count, members - 1)),
            dma((count,)),
        ],
        pltpu.CompilerParams(vmem_limit_bytes=56 * 2**20, collective_id=0, has_side_effects=True),
        [pl.BlockSpec(memory_space=pl.ANY), VMEM, VMEM])
    back, = call(
        functools.partial(analysis_kernel, levels), [packed],
        (got, obs_op, obs_value[:, :, None], obs_precision[:, :, None]),
        [
            pltpu.VMEM((patches, entries, ens), F32),
            pltpu.VMEM((patches, entries, 1), F32),
            pltpu.VMEM((patches, nobs, ens), F32),
            pltpu.VMEM((patches, nobs, 1), F32),
            pltpu.VMEM((patches, nobs, 3 * nobs), F32),
            pltpu.VMEM((patches, 8, GY), F32),
        ])
    back = lax.all_to_all(back, "member", split_axis=0, concat_axis=0, tiled=True)
    return call(unpack_kernel, [ensemble.shape], (back,))[0]


def solution(mesh):
    return jax.shard_map(
        shards,
        mesh=mesh,
        in_specs=(
            P("member", None, "region"),
            P(),
            P(),
            P(("region", "member"), None, None),
            P(("region", "member"), None),
            P(("region", "member"), None),
        ),
        out_specs=P("member", None, "region"),
        check_vma=False,
    )
```

```python
import functools
import math

import jax
import jax.numpy as jnp
from jax import lax
from jax.experimental import pallas as pl
from jax.experimental.pallas import tpu as pltpu
from jax.sharding import PartitionSpec as P

GY = 128
NSTEP = 4
ITERS = 12
HIGHEST = lax.Precision.HIGHEST
F32 = jnp.float32
BF16 = jnp.bfloat16
VMEM = pl.BlockSpec(memory_space=pltpu.VMEM)
PARAMS = pltpu.CompilerParams(vmem_limit_bytes=56 * 2**20)


def mm(a, b):
    return jnp.dot(a, b, preferred_element_type=F32)


def split2(x):
    hi = x.astype(BF16)
    return hi, (x - hi.astype(F32)).astype(BF16)


def split3(x):
    hi = x.astype(BF16)
    rest = x - hi.astype(F32)
    mid = rest.astype(BF16)
    return hi, mid, (rest - mid.astype(F32)).astype(BF16)


def dot3(a, b):
    a0, a1 = split2(a)
    b0, b1 = split2(b)
    return mm(a0, b0) + (mm(a0, b1) + mm(a1, b0))


def dot6(a, b):
    a0, a1, a2 = split3(a)
    b0, b1, b2 = split3(b)
    left = jnp.concatenate([a0, a1], 1)
    low = mm(jnp.concatenate([a0, a2], 1), jnp.concatenate([b2, b0], 0))
    low = low + mm(left, jnp.concatenate([b1, b0], 0))
    return low + mm(left, jnp.concatenate([b0, b1], 0))


def mixing(blend_ref, levels):
    padded = blend_ref.shape[0]
    hi, lo = split2(blend_ref[...])
    lane = lax.broadcasted_iota(jnp.int32, blend_ref.shape, 1)
    return jnp.where(lane < 2 * padded, hi.astype(F32), lo.astype(F32)).astype(BF16)


def advance(parts, mix, rate):
    x = jnp.concatenate(parts, 1)
    levels = x.shape[0]
    padded = mix.shape[0]
    full = jnp.concatenate([x, jnp.zeros((padded - levels, x.shape[1]), F32)], 0)
    hi, lo = split2(full)
    coupled = mm(mix, jnp.concatenate([hi, lo, hi], 0))[:levels]
    rows = len(parts)
    out = []
    for r in range(rows):
        c = parts[r]
        lap = pltpu.roll(c, 1, 1) + pltpu.roll(c, GY - 1, 1) - 4.0 * c
        if r:
            lap = lap + parts[r - 1]
        if r < rows - 1:
            lap = lap + parts[r + 1]
        out.append(c + rate * lap + 0.3 * jnp.tanh(coupled[:, r * GY:(r + 1) * GY]))
    return out


def rows_of(i, levels, stride):
    return pl.ds(0, levels) if stride == 1 else pl.ds(i, levels, stride=stride)


def groups_of(group):
    count = max(1, group // 8)
    return count, group // count


def others(axis):
    count = lax.axis_size(axis)
    me = lax.axis_index(axis)
    return me, [lax.rem(me + j, count) for j in range(1, count)]


def swap_blocks(tiles):
    count = len(tiles)
    width = GY // count
    block = lax.broadcasted_iota(jnp.int32, tiles[0].shape, 1) // width
    bit = 1
    while bit < count:
        low = lax.rem(block // bit, 2) == 0
        out = list(tiles)
        for k in range(count):
            if not k & bit:
                a, b = tiles[k], tiles[k | bit]
                out[k] = jnp.where(low, a, pltpu.roll(b, bit * width, 1))
                out[k | bit] = jnp.where(low, pltpu.roll(a, GY - bit * width, 1), b)
        tiles = out
        bit *= 2
    return tiles


def each(total, unroll, body):
    trips = total // unroll
    if trips:
        @pl.loop(0, trips)
        def _(i):
            for d in range(unroll):
                body(i * unroll + d)
    for d in range(trips * unroll, total):
        body(d)


def tile_rows(f, size):
    return pl.ds(f, 1) if size == 1 else pl.ds(pl.multiple_of(f * size, size), size)


def forecast_kernel(ens_ref, blend_ref, rate_ref, o_ref, x_ref, up_ref, down_ref, pack_ref, rate_rows,
                    halo_send, halo_recv, part_send, part_recv, own_sem):
    _, rows, count, pack, packed, _ = x_ref.shape
    levels = ens_ref.shape[0]
    size = packed // levels
    members = lax.axis_size("member")
    me, peers = others("member")
    regions = lax.axis_size("region")
    here = lax.axis_index("region")
    above = lax.rem(here + 1, regions)
    below = lax.rem(here + regions - 1, regions)

    barrier = pltpu.get_barrier_semaphore()
    for other in peers:
        pl.semaphore_signal(barrier, inc=1, device_id={"member": other},
                            device_id_type=pl.DeviceIdType.MESH)
    for other in (above, below):
        pl.semaphore_signal(barrier, inc=1, device_id={"region": other},
                            device_id_type=pl.DeviceIdType.MESH)

    def halos(k, g):
        return [
            pltpu.make_async_remote_copy(
                src_ref=x_ref.at[k % 2, r, g], dst_ref=ref.at[k, g],
                send_sem=halo_send.at[side, k, g], recv_sem=halo_recv.at[side, k, g],
                device_id={"region": other}, device_id_type=pl.DeviceIdType.MESH)
            for side, (r, ref, other) in enumerate(
                ((rows - 1, up_ref, above), (0, down_ref, below)))
        ]

    def part(g, d):
        return pltpu.make_async_remote_copy(
            src_ref=pack_ref.at[d, g], dst_ref=o_ref.at[me, g],
            send_sem=part_send.at[g, d], recv_sem=part_recv.at[g, me],
            device_id={"member": d}, device_id_type=pl.DeviceIdType.MESH)

    def arrival(g, d):
        return pltpu.make_async_remote_copy(
            src_ref=pack_ref.at[d, g], dst_ref=o_ref.at[d, g],
            send_sem=part_send.at[g, d], recv_sem=part_recv.at[g, d],
            device_id={"member": d}, device_id_type=pl.DeviceIdType.MESH)

    def own(g):
        return pltpu.make_async_copy(pack_ref.at[me, g], o_ref.at[me, g], own_sem.at[g])

    mix = mixing(blend_ref, levels)
    rate = rate_ref[...]

    def load(g):
        def body(f):
            for r in range(rows):
                for h in range(pack):
                    first = (h * count + g) * size
                    x_ref[0, r, g, h, tile_rows(f, size), :] = (
                        ens_ref[f, first:first + size, r * GY:(r + 1) * GY])
        each(levels, 4, body)

    def inner(k, g):
        def body(i):
            place = rows_of(i, levels, size)
            for h in range(pack):
                new = advance([x_ref[k % 2, r, g, h, place, :] for r in range(rows)], mix, rate)
                for r in range(rows):
                    x_ref[(k + 1) % 2, r, g, h, place, :] = new[r]
        each(size, 2, body)

    def border(k, g):
        def body(f):
            place = tile_rows(f, size)
            factor = rate_rows[tile_rows(f, 8), :][:size]
            for h in range(pack):
                for r, ref in ((0, up_ref), (rows - 1, down_ref)):
                    x_ref[(k + 1) % 2, r, g, h, place, :] = (
                        x_ref[(k + 1) % 2, r, g, h, place, :] + factor * ref[k, g, h, place, :])
        each(levels, 4, body)

    def ship(g, chosen):
        def body(f):
            place = tile_rows(f, size)
            for r in chosen:
                tiles = swap_blocks([x_ref[NSTEP % 2, r, g, h, place, :] for h in range(pack)])
                for c in range(pack):
                    pack_ref[r * pack + c, g, place, :] = tiles[c]
        each(levels, 4, body)
        for r in chosen:
            for c in range(pack):
                d = r * pack + c

                @pl.when(me != d)
                def _():
                    part(g, d).start()

    for g in range(count):
        load(g)
        if g == 0:
            pl.semaphore_wait(barrier, len(peers) + 2)
        for copy in halos(0, g):
            copy.start()

    def body(f):
        rate_rows[tile_rows(f, 8), :] = jnp.broadcast_to(rate_ref[pl.ds(f, 1), :], (8, GY))
    each(levels, 4, body)
    for g in range(count):
        inner(0, g)
    for k in range(NSTEP):
        for g in range(count):
            for copy in halos(k, g):
                copy.wait()
            border(k, g)
            if k < NSTEP - 1:
                for copy in halos(k + 1, g):
                    copy.start()
                inner(k + 1, g)
                if k + 1 == NSTEP - 1:
                    ship(g, range(1, rows - 1))
            else:
                ship(g, sorted({0, rows - 1}))
                own(g).start()
    for g in range(count):
        for d in range(members):
            @pl.when(me != d)
            def _():
                part(g, d).wait_send()
                arrival(g, d).wait_recv()
        own(g).wait()


def unpack_kernel(chunk, x_ref, o_ref):
    sets, _, count, packed, _ = x_ref.shape
    mem, cols = o_ref.shape[2:]
    rows = cols // GY
    pack = x_ref.shape[1] // rows
    size = mem // (pack * count)

    def body(f):
        for g in range(count):
            for r in range(rows):
                tiles = swap_blocks([x_ref[c, r * pack + k, g, tile_rows(f, size), :]
                                     for k in range(pack) for c in range(sets)])
                for part in range(sets):
                    for h in range(pack):
                        first = (h * count + g) * size
                        o_ref[part, f, first:first + size, r * GY:(r + 1) * GY] = (
                            tiles[part * pack + h])
    each(chunk, 1, body)


def analysis_kernel(levels, x_ref, op_ref, val_ref, prec_ref, o_ref,
                    xt_ref, mean_ref, u_ref, v_ref, state_ref, scal_ref,
                    send_ref, send_sem, recv_sem, own_sem):
    sources, count, packed, _ = x_ref.shape
    size = packed // levels
    patches, entries, nobs = op_ref.shape
    sets = o_ref.shape[0]
    per_set = patches // sets
    chunk = levels // sets
    batches = 2
    per_batch = patches // batches
    me, peers = others("member")
    cells = entries // levels
    ens = xt_ref.shape[2]
    width = patches * cells
    pack = GY // width
    share = sources * size
    half = count * share
    a = ens - 1.0
    eye = (lax.broadcasted_iota(jnp.int32, (nobs, nobs), 0)
           == lax.broadcasted_iota(jnp.int32, (nobs, nobs), 1)).astype(F32)

    barrier = pltpu.get_barrier_semaphore()
    for other in peers:
        pl.semaphore_signal(barrier, inc=1, device_id={"member": other},
                            device_id_type=pl.DeviceIdType.MESH)

    def part(c, j):
        return pltpu.make_async_remote_copy(
            src_ref=send_ref.at[c, peers[j]], dst_ref=o_ref.at[c, me],
            send_sem=send_sem.at[c, j], recv_sem=recv_sem.at[c, j],
            device_id={"member": peers[j]}, device_id_type=pl.DeviceIdType.MESH)

    def own(c):
        return pltpu.make_async_copy(send_ref.at[c, me], o_ref.at[c, me], own_sem.at[c])

    def column(row):
        return jnp.sum(eye * row, axis=1, keepdims=True)

    def spread(f):
        if size == 1:
            x = [x_ref[:, g, f, :] for g in range(count)]
        else:
            x = [x_ref[:, g, tile_rows(f, size), :].reshape(share, GY) for g in range(count)]
        t = jnp.concatenate(x, 0).T
        for h in range(pack):
            for p in range(patches):
                xt_ref[p, tile_rows(f, cells), h * half:(h + 1) * half] = (
                    t[h * width + p * cells:h * width + (p + 1) * cells, :])
    each(levels, 4, spread)

    for b in range(batches):
        start = b * per_batch

        @pl.loop(start, start + per_batch)
        def _(p):
            x = xt_ref[p]
            mean = jnp.sum(x, axis=1, keepdims=True) * (1.0 / ens)
            e = x - mean
            xt_ref[p] = e
            mean_ref[p] = mean
            op = op_ref[p]
            obs_mean = jnp.sum(op * mean, axis=0, keepdims=True)
            root = jnp.sqrt(prec_ref[pl.ds(p, 1), :])
            u = dot3(op.T, e) * column(root)
            u_ref[p] = u
            v_ref[p] = root * (val_ref[pl.ds(p, 1), :] - obs_mean)
            gram = lax.dot_general(u, u, (((1,), (1,)), ((), ())), precision=HIGHEST,
                                   preferred_element_type=F32)
            trace = jnp.sum(u * u, keepdims=True).reshape(1, 1)
            square = jnp.sum(gram * gram, keepdims=True).reshape(1, 1)
            s = jnp.sqrt(a * a * ens + 2.0 * a * trace + square)
            alpha = a / s
            state_ref[p, :, 0:nobs] = alpha * eye + gram / s
            state_ref[p, :, nobs:2 * nobs] = eye
            state_ref[p, :, 2 * nobs:3 * nobs] = jnp.zeros_like(eye)
            scal_ref[p, 0:1, :] = jnp.broadcast_to(s, (1, GY))
            scal_ref[p, 1:2, :] = jnp.broadcast_to(alpha, (1, GY))
            scal_ref[p, 2:3, :] = jnp.ones((1, GY), F32)

        @pl.loop(0, ITERS)
        def _(k):
            firsts = {}
            for p in range(start, start + per_batch):
                state = state_ref[p]
                firsts[p] = dot6(state[:, nobs:2 * nobs], state)
            for p in range(start, start + per_batch):
                first = firsts[p]
                alpha = scal_ref[p, 1:2, 0:1]
                z = scal_ref[p, 2:3, 0:1]
                factor = 1.5 * eye - 0.5 * first[:, 0:nobs]
                second = dot6(factor, state_ref[p])
                state_ref[p, :, 0:2 * nobs] = second[:, 0:2 * nobs]
                q = state_ref[p, :, 2 * nobs:3 * nobs]
                state_ref[p, :, 2 * nobs:3 * nobs] = second[:, 2 * nobs:3 * nobs] - 0.5 * z * (
                    first[:, nobs:2 * nobs] + alpha * (first[:, 2 * nobs:3 * nobs] + z * q))
                scal_ref[p, 2:3, :] = jnp.broadcast_to(z * (1.5 - 0.5 * alpha * z * z), (1, GY))

        for c in range(b * sets // batches, (b + 1) * sets // batches):
            @pl.loop(c * per_set, (c + 1) * per_set)
            def _(p):
                s = scal_ref[p, 0:1, 0:1]
                z = scal_ref[p, 2:3, 0:1]
                scale = lax.rsqrt(s)
                root = state_ref[p, :, nobs:2 * nobs] * scale
                u = u_ref[p]
                once = jnp.sum(root * column(v_ref[p]), axis=0, keepdims=True)
                twice = jnp.sum(root * once, axis=1, keepdims=True)
                w = jnp.sum(u * twice, axis=0, keepdims=True)
                e = xt_ref[p]
                qu = dot3(state_ref[p, :, 2 * nobs:3 * nobs], u) * (math.sqrt(a) * scale / s)
                weights = dot3(u.T, qu)
                shift = mean_ref[p] + jnp.sum(e * w, axis=1, keepdims=True)
                xt_ref[p] = shift + (math.sqrt(a) * scale * z) * e + dot3(e, weights)

            def collect(f):
                t = jnp.concatenate([
                    xt_ref[p, tile_rows(q * chunk + f, cells), h * half:(h + 1) * half]
                    for q in range(sets) for h in range(pack)
                    for p in range(c * per_set, (c + 1) * per_set)], 0).T
                for g in range(count):
                    mine = t[g * share:(g + 1) * share]
                    if size == 1:
                        send_ref[c, :, g, tile_rows(f, size), :] = mine.reshape(sources, 1, GY)
                    else:
                        send_ref[c, :, g, tile_rows(f, size), :] = mine.reshape(sources, size, GY)
            each(chunk, 4, collect)

            if c == 0:
                pl.semaphore_wait(barrier, len(peers))
            for j in range(len(peers)):
                part(c, j).start()
            own(c).start()

    for c in range(sets):
        for j in range(len(peers)):
            part(c, j).wait()
        own(c).wait()


def remote_params(collective_id):
    return pltpu.CompilerParams(vmem_limit_bytes=56 * 2**20, collective_id=collective_id,
                                has_side_effects=True)


def call(kernel, outs, args, scratch=(), params=PARAMS):
    return pl.pallas_call(
        kernel,
        out_shape=[jax.ShapeDtypeStruct(s, F32) for s in outs],
        in_specs=[VMEM] * len(args),
        out_specs=[VMEM] * len(outs),
        scratch_shapes=list(scratch),
        compiler_params=params,
    )(*args)


def shards(ensemble, blending_matrix, lateral_spreading, obs_op, obs_value, obs_precision):
    mem, levels, cols = ensemble.shape
    members = lax.axis_size("member")
    patches, nobs, entries = obs_op.shape
    ens = mem * members
    rows = cols // GY
    pack = GY * members // cols
    count, size = groups_of(mem // pack)
    padded = -(-levels // 16) * 16
    blend = jnp.tile(jnp.pad(blending_matrix, ((0, padded - levels),) * 2), (1, 3))
    rate = lateral_spreading[:, None]
    packed = (members, count, levels * size, GY)
    dma = pltpu.SemaphoreType.DMA
    got, = call(
        forecast_kernel, [packed], (ensemble.transpose(1, 0, 2), blend, rate),
        [
            pltpu.VMEM((2, rows, count, pack, levels * size, GY), F32),
            pltpu.VMEM((NSTEP, count, pack, levels * size, GY), F32),
            pltpu.VMEM((NSTEP, count, pack, levels * size, GY), F32),
            pltpu.VMEM(packed, F32),
            pltpu.VMEM((levels * 8, GY), F32),
            dma((2, NSTEP, count)),
            dma((2, NSTEP, count)),
            dma((count, members)),
            dma((count, members)),
            dma((count,)),
        ],
        remote_params(0))
    sets = min(4, patches)
    parts = (sets, members, count, levels // sets * size, GY)
    back, = call(
        functools.partial(analysis_kernel, levels), [parts],
        (got, obs_op.transpose(0, 2, 1), obs_value, obs_precision),
        [
            pltpu.VMEM((patches, entries, ens), F32),
            pltpu.VMEM((patches, entries, 1), F32),
            pltpu.VMEM((patches, nobs, ens), F32),
            pltpu.VMEM((patches, 1, nobs), F32),
            pltpu.VMEM((patches, nobs, 3 * nobs), F32),
            pltpu.VMEM((patches, 8, GY), F32),
            pltpu.VMEM(parts, F32),
            dma((sets, members - 1)),
            dma((sets, members - 1)),
            dma((sets,)),
        ],
        remote_params(1))
    chunk = levels // sets
    steps = chunk if size % 8 == 0 else 1
    out = pl.pallas_call(
        functools.partial(unpack_kernel, chunk // steps),
        out_shape=jax.ShapeDtypeStruct((sets, chunk, mem, cols), F32),
        grid=(steps,),
        in_specs=[pl.BlockSpec((sets, members, count, chunk // steps * size, GY),
                               lambda i: (0, 0, 0, i, 0))],
        out_specs=pl.BlockSpec((sets, chunk // steps, mem, cols), lambda i: (0, i, 0, 0)),
        compiler_params=PARAMS,
    )(back)
    return out.reshape(levels, mem, cols).transpose(1, 0, 2)


def solution(mesh):
    return jax.shard_map(
        shards,
        mesh=mesh,
        in_specs=(
            P("member", None, "region"),
            P(),
            P(),
            P(("region", "member"), None, None),
            P(("region", "member"), None),
            P(("region", "member"), None),
        ),
        out_specs=P("member", None, "region"),
        check_vma=False,
    )
```

```python
import functools
import math

import jax
import jax.numpy as jnp
from jax import lax
from jax.experimental import pallas as pl
from jax.experimental.pallas import tpu as pltpu
from jax.sharding import PartitionSpec as P

GY = 128
NSTEP = 4
ITERS = 12
HIGHEST = lax.Precision.HIGHEST
F32 = jnp.float32
BF16 = jnp.bfloat16
VMEM = pl.BlockSpec(memory_space=pltpu.VMEM)
PARAMS = pltpu.CompilerParams(vmem_limit_bytes=56 * 2**20)


def mm(a, b):
    return jnp.dot(a, b, preferred_element_type=F32)


def split2(x):
    hi = x.astype(BF16)
    return hi, (x - hi.astype(F32)).astype(BF16)


def split3(x):
    hi = x.astype(BF16)
    rest = x - hi.astype(F32)
    mid = rest.astype(BF16)
    return hi, mid, (rest - mid.astype(F32)).astype(BF16)


def dot3(a, b):
    a0, a1 = split2(a)
    b0, b1 = split2(b)
    return mm(a0, b0) + (mm(a0, b1) + mm(a1, b0))


def dot6(a, b):
    a0, a1, a2 = split3(a)
    b0, b1, b2 = split3(b)
    left = jnp.concatenate([a0, a1], 1)
    low = mm(jnp.concatenate([a0, a2], 1), jnp.concatenate([b2, b0], 0))
    low = low + mm(left, jnp.concatenate([b1, b0], 0))
    return low + mm(left, jnp.concatenate([b0, b1], 0))


def mixing(blend_ref, levels):
    padded = blend_ref.shape[0]
    hi, lo = split2(blend_ref[...])
    lane = lax.broadcasted_iota(jnp.int32, blend_ref.shape, 1)
    return jnp.where(lane < 2 * padded, hi.astype(F32), lo.astype(F32)).astype(BF16)


def advance(parts, mix, rate):
    x = jnp.concatenate(parts, 1)
    levels = x.shape[0]
    padded = mix.shape[0]
    full = jnp.concatenate([x, jnp.zeros((padded - levels, x.shape[1]), F32)], 0)
    hi, lo = split2(full)
    coupled = mm(mix, jnp.concatenate([hi, lo, hi], 0))[:levels]
    rows = len(parts)
    out = []
    for r in range(rows):
        c = parts[r]
        lap = pltpu.roll(c, 1, 1) + pltpu.roll(c, GY - 1, 1) - 4.0 * c
        if r:
            lap = lap + parts[r - 1]
        if r < rows - 1:
            lap = lap + parts[r + 1]
        out.append(c + rate * lap + 0.3 * jnp.tanh(coupled[:, r * GY:(r + 1) * GY]))
    return out


def rows_of(i, levels, stride):
    return pl.ds(0, levels) if stride == 1 else pl.ds(i, levels, stride=stride)


def groups_of(group):
    count = max(1, group // 8)
    return count, group // count


def others(axis):
    count = lax.axis_size(axis)
    me = lax.axis_index(axis)
    return me, [lax.rem(me + j, count) for j in range(1, count)]


def swap_blocks(tiles):
    count = len(tiles)
    width = GY // count
    block = lax.broadcasted_iota(jnp.int32, tiles[0].shape, 1) // width
    bit = 1
    while bit < count:
        low = lax.rem(block // bit, 2) == 0
        out = list(tiles)
        for k in range(count):
            if not k & bit:
                a, b = tiles[k], tiles[k | bit]
                out[k] = jnp.where(low, a, pltpu.roll(b, bit * width, 1))
                out[k | bit] = jnp.where(low, pltpu.roll(a, GY - bit * width, 1), b)
        tiles = out
        bit *= 2
    return tiles


def each(total, unroll, body):
    trips = total // unroll
    if trips:
        @pl.loop(0, trips)
        def _(i):
            for d in range(unroll):
                body(i * unroll + d)
    for d in range(trips * unroll, total):
        body(d)


def tile_rows(f, size):
    return pl.ds(f, 1) if size == 1 else pl.ds(pl.multiple_of(f * size, size), size)


def forecast_kernel(ens_ref, blend_ref, rate_ref, o_ref, x_ref, up_ref, down_ref, pack_ref, rate_rows,
                    halo_send, halo_recv, part_send, part_recv, own_sem):
    _, rows, count, pack, packed, _ = x_ref.shape
    levels = ens_ref.shape[0]
    size = packed // levels
    members = lax.axis_size("member")
    me, peers = others("member")
    regions = lax.axis_size("region")
    here = lax.axis_index("region")
    above = lax.rem(here + 1, regions)
    below = lax.rem(here + regions - 1, regions)

    barrier = pltpu.get_barrier_semaphore()
    for other in peers:
        pl.semaphore_signal(barrier, inc=1, device_id={"member": other},
                            device_id_type=pl.DeviceIdType.MESH)
    for other in (above, below):
        pl.semaphore_signal(barrier, inc=1, device_id={"region": other},
                            device_id_type=pl.DeviceIdType.MESH)

    def halos(k, g):
        return [
            pltpu.make_async_remote_copy(
                src_ref=x_ref.at[k % 2, r, g], dst_ref=ref.at[k, g],
                send_sem=halo_send.at[side, k, g], recv_sem=halo_recv.at[side, k, g],
                device_id={"region": other}, device_id_type=pl.DeviceIdType.MESH)
            for side, (r, ref, other) in enumerate(
                ((rows - 1, up_ref, above), (0, down_ref, below)))
        ]

    def part(g, d):
        return pltpu.make_async_remote_copy(
            src_ref=pack_ref.at[d, g], dst_ref=o_ref.at[me, g],
            send_sem=part_send.at[g, d], recv_sem=part_recv.at[g, me],
            device_id={"member": d}, device_id_type=pl.DeviceIdType.MESH)

    def arrival(g, d):
        return pltpu.make_async_remote_copy(
            src_ref=pack_ref.at[d, g], dst_ref=o_ref.at[d, g],
            send_sem=part_send.at[g, d], recv_sem=part_recv.at[g, d],
            device_id={"member": d}, device_id_type=pl.DeviceIdType.MESH)

    def own(g):
        return pltpu.make_async_copy(pack_ref.at[me, g], o_ref.at[me, g], own_sem.at[g])

    mix = mixing(blend_ref, levels)
    rate = rate_ref[...]

    def load(g):
        def body(f):
            for r in range(rows):
                for h in range(pack):
                    first = (h * count + g) * size
                    x_ref[0, r, g, h, tile_rows(f, size), :] = (
                        ens_ref[f, first:first + size, r * GY:(r + 1) * GY])
        each(levels, 4, body)

    def inner(k, g):
        def body(i):
            place = rows_of(i, levels, size)
            for h in range(pack):
                new = advance([x_ref[k % 2, r, g, h, place, :] for r in range(rows)], mix, rate)
                for r in range(rows):
                    x_ref[(k + 1) % 2, r, g, h, place, :] = new[r]
        each(size, 2, body)

    def border(k, g):
        def body(f):
            place = tile_rows(f, size)
            factor = rate_rows[tile_rows(f, 8), :][:size]
            for h in range(pack):
                for r, ref in ((0, up_ref), (rows - 1, down_ref)):
                    x_ref[(k + 1) % 2, r, g, h, place, :] = (
                        x_ref[(k + 1) % 2, r, g, h, place, :] + factor * ref[k, g, h, place, :])
        each(levels, 4, body)

    def ship(g, chosen):
        def body(f):
            place = tile_rows(f, size)
            for r in chosen:
                tiles = swap_blocks([x_ref[NSTEP % 2, r, g, h, place, :] for h in range(pack)])
                for c in range(pack):
                    pack_ref[r * pack + c, g, place, :] = tiles[c]
        each(levels, 4, body)
        for r in chosen:
            for c in range(pack):
                d = r * pack + c

                @pl.when(me != d)
                def _():
                    part(g, d).start()

    for g in range(count):
        load(g)
        if g == 0:
            pl.semaphore_wait(barrier, len(peers) + 2)
        for copy in halos(0, g):
            copy.start()

    def body(f):
        rate_rows[tile_rows(f, 8), :] = jnp.broadcast_to(rate_ref[pl.ds(f, 1), :], (8, GY))
    each(levels, 4, body)
    for g in range(count):
        inner(0, g)
    for k in range(NSTEP):
        for g in range(count):
            for copy in halos(k, g):
                copy.wait()
            border(k, g)
            if k < NSTEP - 1:
                for copy in halos(k + 1, g):
                    copy.start()
                inner(k + 1, g)
                if k + 1 == NSTEP - 1:
                    ship(g, range(1, rows - 1))
            else:
                ship(g, sorted({0, rows - 1}))
                own(g).start()
    for g in range(count):
        for d in range(members):
            @pl.when(me != d)
            def _():
                part(g, d).wait_send()
                arrival(g, d).wait_recv()
        own(g).wait()


def unpack_kernel(x_ref, o_ref):
    sets, pack, count, _, _ = x_ref.shape
    _, chunk, mem, _ = o_ref.shape
    size = mem // (pack * count)

    def body(f):
        for g in range(count):
            tiles = swap_blocks([x_ref[c, k, g, tile_rows(f, size), :]
                                 for k in range(pack) for c in range(sets)])
            for part in range(sets):
                for h in range(pack):
                    first = (h * count + g) * size
                    o_ref[part, f, first:first + size, :] = tiles[part * pack + h]
    each(chunk, 4, body)


def analysis_kernel(levels, x_ref, op_ref, val_ref, prec_ref, o_ref,
                    xt_ref, mean_ref, u_ref, v_ref, state_ref, scal_ref,
                    send_ref, send_sem, recv_sem, own_sem):
    sources, count, packed, _ = x_ref.shape
    size = packed // levels
    patches, entries, nobs = op_ref.shape
    sets = o_ref.shape[0]
    per_set = patches // sets
    chunk = levels // sets
    batches = sets
    per_batch = patches // batches
    me, peers = others("member")
    cells = entries // levels
    ens = xt_ref.shape[2]
    width = patches * cells
    pack = GY // width
    share = sources * size
    half = count * share
    a = ens - 1.0
    eye = (lax.broadcasted_iota(jnp.int32, (nobs, nobs), 0)
           == lax.broadcasted_iota(jnp.int32, (nobs, nobs), 1)).astype(F32)

    barrier = pltpu.get_barrier_semaphore()
    for other in peers:
        pl.semaphore_signal(barrier, inc=1, device_id={"member": other},
                            device_id_type=pl.DeviceIdType.MESH)

    def part(c, j):
        return pltpu.make_async_remote_copy(
            src_ref=send_ref.at[c, peers[j]], dst_ref=o_ref.at[c, me],
            send_sem=send_sem.at[c, j], recv_sem=recv_sem.at[c, j],
            device_id={"member": peers[j]}, device_id_type=pl.DeviceIdType.MESH)

    def own(c):
        return pltpu.make_async_copy(send_ref.at[c, me], o_ref.at[c, me], own_sem.at[c])

    def column(row):
        return jnp.sum(eye * row, axis=1, keepdims=True)

    def spread(f):
        if size == 1:
            x = [x_ref[:, g, f, :] for g in range(count)]
        else:
            x = [x_ref[:, g, tile_rows(f, size), :].reshape(share, GY) for g in range(count)]
        t = jnp.concatenate(x, 0).T
        for h in range(pack):
            for p in range(patches):
                xt_ref[p, tile_rows(f, cells), h * half:(h + 1) * half] = (
                    t[h * width + p * cells:h * width + (p + 1) * cells, :])
    each(levels, 4, spread)

    for b in range(batches):
        start = b * per_batch

        @pl.loop(start, start + per_batch)
        def _(p):
            x = xt_ref[p]
            mean = jnp.sum(x, axis=1, keepdims=True) * (1.0 / ens)
            e = x - mean
            xt_ref[p] = e
            mean_ref[p] = mean
            op = op_ref[p]
            obs_mean = jnp.sum(op * mean, axis=0, keepdims=True)
            root = jnp.sqrt(prec_ref[pl.ds(p, 1), :])
            u = dot3(op.T, e) * column(root)
            u_ref[p] = u
            v_ref[p] = root * (val_ref[pl.ds(p, 1), :] - obs_mean)
            gram = lax.dot_general(u, u, (((1,), (1,)), ((), ())), precision=HIGHEST,
                                   preferred_element_type=F32)
            trace = jnp.sum(u * u, keepdims=True).reshape(1, 1)
            square = jnp.sum(gram * gram, keepdims=True).reshape(1, 1)
            s = jnp.sqrt(a * a * ens + 2.0 * a * trace + square)
            alpha = a / s
            system = alpha * eye + gram / s
            factor = 1.5 * eye - 0.5 * system
            state_ref[p, :, 0:nobs] = dot6(factor, system)
            state_ref[p, :, nobs:2 * nobs] = factor
            state_ref[p, :, 2 * nobs:3 * nobs] = -0.5 * eye
            scal_ref[p, 0:1, :] = jnp.broadcast_to(s, (1, GY))
            scal_ref[p, 1:2, :] = jnp.broadcast_to(alpha, (1, GY))
            scal_ref[p, 2:3, :] = jnp.broadcast_to(1.5 - 0.5 * alpha, (1, GY))

        @pl.loop(1, ITERS)
        def _(k):
            firsts = {}
            for p in range(start, start + per_batch):
                state = state_ref[p, :, 0:2 * nobs]
                firsts[p] = dot6(state[:, nobs:2 * nobs], state)
            for p in range(start, start + per_batch):
                first = firsts[p]
                alpha = scal_ref[p, 1:2, 0:1]
                z = scal_ref[p, 2:3, 0:1]
                factor = 1.5 * eye - 0.5 * first[:, 0:nobs]
                inv = state_ref[p, :, nobs:2 * nobs]
                mixed = factor - (0.5 * alpha * z) * (inv + z * eye)
                q = dot6(mixed, state_ref[p, :, 2 * nobs:3 * nobs]) - (0.5 * z) * first[:, nobs:2 * nobs]
                state_ref[p, :, 0:2 * nobs] = dot6(factor, state_ref[p, :, 0:2 * nobs])
                state_ref[p, :, 2 * nobs:3 * nobs] = q
                scal_ref[p, 2:3, :] = jnp.broadcast_to(z * (1.5 - 0.5 * alpha * z * z), (1, GY))

        for c in range(b * sets // batches, (b + 1) * sets // batches):
            @pl.loop(c * per_set, (c + 1) * per_set)
            def _(p):
                s = scal_ref[p, 0:1, 0:1]
                z = scal_ref[p, 2:3, 0:1]
                scale = lax.rsqrt(s)
                root = state_ref[p, :, nobs:2 * nobs] * scale
                u = u_ref[p]
                once = jnp.sum(root * column(v_ref[p]), axis=0, keepdims=True)
                twice = jnp.sum(root * once, axis=1, keepdims=True)
                w = jnp.sum(u * twice, axis=0, keepdims=True)
                e = xt_ref[p]
                qu = dot3(state_ref[p, :, 2 * nobs:3 * nobs], u) * (math.sqrt(a) * scale / s)
                weights = dot3(u.T, qu)
                shift = mean_ref[p] + jnp.sum(e * w, axis=1, keepdims=True)
                xt_ref[p] = shift + (math.sqrt(a) * scale * z) * e + dot3(e, weights)

            def collect(f):
                t = jnp.concatenate([
                    xt_ref[p, tile_rows(q * chunk + f, cells), h * half:(h + 1) * half]
                    for q in range(sets) for h in range(pack)
                    for p in range(c * per_set, (c + 1) * per_set)], 0).T
                for g in range(count):
                    mine = t[g * share:(g + 1) * share]
                    if size == 1:
                        send_ref[c, :, g, tile_rows(f, size), :] = mine.reshape(sources, 1, GY)
                    else:
                        send_ref[c, :, g, tile_rows(f, size), :] = mine.reshape(sources, size, GY)
            each(chunk, 4, collect)

            if c == 0:
                pl.semaphore_wait(barrier, len(peers))
            for j in range(len(peers)):
                part(c, j).start()
            own(c).start()

    for c in range(sets):
        for j in range(len(peers)):
            part(c, j).wait()
        own(c).wait()


def remote_params(collective_id):
    return pltpu.CompilerParams(vmem_limit_bytes=56 * 2**20, collective_id=collective_id,
                                has_side_effects=True)


def call(kernel, outs, args, scratch=(), params=PARAMS):
    return pl.pallas_call(
        kernel,
        out_shape=[jax.ShapeDtypeStruct(s, F32) for s in outs],
        in_specs=[VMEM] * len(args),
        out_specs=[VMEM] * len(outs),
        scratch_shapes=list(scratch),
        compiler_params=params,
    )(*args)


def shards(ensemble, blending_matrix, lateral_spreading, obs_op, obs_value, obs_precision):
    mem, levels, cols = ensemble.shape
    members = lax.axis_size("member")
    patches, nobs, entries = obs_op.shape
    ens = mem * members
    rows = cols // GY
    pack = GY * members // cols
    count, size = groups_of(mem // pack)
    padded = -(-levels // 16) * 16
    blend = jnp.tile(jnp.pad(blending_matrix, ((0, padded - levels),) * 2), (1, 3))
    rate = lateral_spreading[:, None]
    packed = (members, count, levels * size, GY)
    dma = pltpu.SemaphoreType.DMA
    got, = call(
        forecast_kernel, [packed], (ensemble.transpose(1, 0, 2), blend, rate),
        [
            pltpu.VMEM((2, rows, count, pack, levels * size, GY), F32),
            pltpu.VMEM((NSTEP, count, pack, levels * size, GY), F32),
            pltpu.VMEM((NSTEP, count, pack, levels * size, GY), F32),
            pltpu.VMEM(packed, F32),
            pltpu.VMEM((levels * 8, GY), F32),
            dma((2, NSTEP, count)),
            dma((2, NSTEP, count)),
            dma((count, members)),
            dma((count, members)),
            dma((count,)),
        ],
        remote_params(0))
    sets = min(4, patches)
    parts = (sets, members, count, levels // sets * size, GY)
    back, = call(
        functools.partial(analysis_kernel, levels), [parts],
        (got, obs_op.transpose(0, 2, 1), obs_value, obs_precision),
        [
            pltpu.VMEM((patches, entries, ens), F32),
            pltpu.VMEM((patches, entries, 1), F32),
            pltpu.VMEM((patches, nobs, ens), F32),
            pltpu.VMEM((patches, 1, nobs), F32),
            pltpu.VMEM((patches, nobs, 3 * nobs), F32),
            pltpu.VMEM((patches, 8, GY), F32),
            pltpu.VMEM(parts, F32),
            dma((sets, members - 1)),
            dma((sets, members - 1)),
            dma((sets,)),
        ],
        remote_params(1))
    chunk = levels // sets
    out = pl.pallas_call(
        unpack_kernel,
        out_shape=jax.ShapeDtypeStruct((sets, chunk, mem, cols), F32),
        grid=(rows,),
        in_specs=[pl.BlockSpec((sets, pack, count, chunk * size, GY), lambda r: (0, r, 0, 0, 0))],
        out_specs=pl.BlockSpec((sets, chunk, mem, GY), lambda r: (0, 0, 0, r)),
        compiler_params=PARAMS,
    )(back)
    return out.reshape(levels, mem, cols).transpose(1, 0, 2)


def solution(mesh):
    return jax.shard_map(
        shards,
        mesh=mesh,
        in_specs=(
            P("member", None, "region"),
            P(),
            P(),
            P(("region", "member"), None, None),
            P(("region", "member"), None),
            P(("region", "member"), None),
        ),
        out_specs=P("member", None, "region"),
        check_vma=False,
    )
```
